32 devices in a mesh: tok: 4 (over x, core), wa: 8 (over z, y).
Axes of the slice: x: 2, y: 2, z: 4, core: 2. Of those that a mesh axis runs over, the one named last changes fastest.
Arguments:
- tokens: bfloat16 [2048, 8192], P('tok', 'wa'), may hold values from -6 to 6
- gate_weight: bfloat16 [224, 8, 128, 128], P('wa', 'tok'), may hold values from -0.1875 to 0.1875
- up_weight: bfloat16 [224, 8, 128, 128], P('wa', 'tok'), may hold values from -0.1875 to 0.1875
- down_weight: bfloat16 [64, 24, 128, 128], P('wa', 'tok'), may hold values from -0.109375 to 0.109375
- gate_list: int32 [224, 8], P('wa'), may hold values from -1 to 63, as said below
- up_list: int32 [224, 8], P('wa'), may hold values from -1 to 63, as said below
- down_list: int32 [64, 24], replicated, may hold values from -1 to 223, as said below
Outputs:
- mixed_out: bfloat16 [2048, 8192], P('tok', 'wa')
The draws below stay inside these ranges and needn't reach their ends.
Inputs may be any that keep to these rules, and one draw needn't show every extreme that they name: `gate_list`: row j lists distinct feature blocks in ascending order followed by -1; each row has 4 to 8 entries and some row exactly 8. `up_list`: row j lists distinct feature blocks in ascending order followed by -1; each row has 4 to 8 entries and some row exactly 8. `down_list`: row c lists distinct hidden blocks in ascending order followed by -1; each row has 18 to 24 entries and some row exactly 24. Each aligned group of 8 rows names at most 4 distinct blocks of any aligned range of 28 hidden blocks, and every group names exactly 4 of some range.
All inputs are finite; a program needn't handle non-finite values.
Results may differ from the reference program's by a relative error of at most 0.0049.
Values may be sent and summed in bfloat16 or wider, within the bound.
A program may use at most 192 MiB of HBM per device.

```python
import jax
import jax.numpy as jnp
from jax import lax

D = 8192
BLK = 128
KG = 8
KD = 24
TOKENS = 2048
ROWB = 64
HIDB = 224
HB_DEV = 28
DB_DEV = 8
CAP = 4


def column_lists(key, columns, choices, width):
    score_key, count_key = jax.random.split(key)
    scores = jax.random.randint(score_key, (columns, choices), 0, 1 << 20) * choices
    scores = scores + jnp.arange(choices, dtype=jnp.int32)[None, :]
    top_values, chosen = lax.top_k(scores, width)
    chosen = jnp.sort(chosen.astype(jnp.int32), axis=1)
    counts = jax.random.randint(count_key, (columns,), width // 2, width + 1)
    counts = counts.at[0].set(width)
    keep = jnp.arange(width, dtype=jnp.int32)[None, :] < counts[:, None]
    return jnp.where(keep, chosen, -1).astype(jnp.int32)


def draw_gate_list(key, part):
    return column_lists(jax.random.fold_in(key, 11), HIDB, ROWB, KG)


def draw_up_list(key, part):
    return column_lists(jax.random.fold_in(key, 12), HIDB, ROWB, KG)


def draw_down_list(key, part):
    owners = HIDB // HB_DEV
    groups = ROWB // DB_DEV
    pool_key, pick_key, count_key = jax.random.split(jax.random.fold_in(key, 13), 3)
    pool_scores = jax.random.randint(pool_key, (groups, owners, HB_DEV), 0, 1 << 20) * HB_DEV
    pool_scores = pool_scores + jnp.arange(HB_DEV, dtype=jnp.int32)[None, None, :]
    pool_values, local_ids = lax.top_k(pool_scores, CAP)
    owner_base = jnp.arange(owners, dtype=jnp.int32)[None, :, None] * HB_DEV
    pool = (local_ids.astype(jnp.int32) + owner_base).reshape(groups, owners * CAP)
    pool_size = owners * CAP
    forced = (jnp.arange(groups, dtype=jnp.int32) + 1) % owners
    slot_owner = jnp.arange(pool_size, dtype=jnp.int32) // CAP
    first_column = (jnp.arange(DB_DEV, dtype=jnp.int32) == 0)[None, :, None]
    boost = ((slot_owner[None, :] == forced[:, None])[:, None, :] & first_column).astype(jnp.int32)
    scores = jax.random.randint(pick_key, (groups, DB_DEV, pool_size), 0, 1 << 20) * pool_size
    scores = scores + jnp.arange(pool_size, dtype=jnp.int32)[None, None, :] + boost * (1 << 29)
    pick_values, chosen = lax.top_k(scores, KD)
    expanded = jnp.broadcast_to(pool[:, None, :], (groups, DB_DEV, pool_size))
    named = jnp.take_along_axis(expanded, chosen.astype(jnp.int32), axis=2)
    named = jnp.sort(named, axis=2)
    counts = jax.random.randint(count_key, (groups, DB_DEV), 3 * KD // 4, KD + 1)
    counts = counts.at[:, 0].set(KD)
    keep = jnp.arange(KD, dtype=jnp.int32)[None, None, :] < counts[:, :, None]
    return jnp.where(keep, named, -1).reshape(ROWB, KD).astype(jnp.int32)


def levels(own_key, dims, shards, low, high):
    loudness, own = 1.0, jax.random.fold_in(own_key, 6)
    for position, parts in shards:
        steps = jnp.exp(jax.random.uniform(jax.random.fold_in(own, position), (parts,), jnp.float32, low / len(shards), high / len(shards)))
        loudness = loudness * jnp.repeat(steps, dims[position] // parts).reshape([-1 if axis == position else 1 for axis in range(len(dims))])
    return loudness


def scatter_about(own_key, extent, spread, bound, cuts=(), kind=jnp.bfloat16):
    level = levels(own_key, extent, cuts, -0.22, 0.18) if cuts else 1.0
    result = jax.random.normal(own_key, extent, jnp.float32) * spread * level
    return jnp.minimum(jnp.maximum(result, -bound), bound).astype(kind)


def setup_inputs(seed: int = 0) -> dict:
    splits = jax.random.split(jax.random.key(seed), 8)
    tokens = scatter_about(splits[0], (TOKENS, D), 1.0, 6.0, ((0, 4), (1, 8)))
    gate_weight = scatter_about(splits[1], (HIDB, KG, BLK, BLK), (KG * BLK) ** -0.5, 0.1875, ((0, 8), (1, 4)))
    up_weight = scatter_about(splits[2], (HIDB, KG, BLK, BLK), (KG * BLK) ** -0.5, 0.1875, ((0, 8), (1, 4)))
    down_weight = scatter_about(splits[3], (ROWB, KD, BLK, BLK), (KD * BLK) ** -0.5, 0.109375, ((0, 8), (1, 4)))
    gate_list = draw_gate_list(jax.random.fold_in(splits[7], 71), 0)
    up_list = draw_up_list(jax.random.fold_in(splits[7], 71), 0)
    down_list = draw_down_list(jax.random.fold_in(splits[7], 71), 0)
    return {"tokens": tokens, "gate_weight": gate_weight, "up_weight": up_weight, "down_weight": down_weight, "gate_list": gate_list, "up_list": up_list, "down_list": down_list}


def listed_sum(sources, weights, block_list):
    present = (block_list >= 0).astype(jnp.float32)
    picked = jnp.take(sources, jnp.maximum(block_list, 0), axis=0).astype(jnp.float32)
    picked = picked * present[:, None, None]
    return jnp.einsum("ktm,kmn->tn", picked, weights.astype(jnp.float32))


def reference(tokens, gate_weight, up_weight, down_weight, gate_list, up_list, down_list):
    feature_blocks = jnp.transpose(tokens.reshape(TOKENS, ROWB, BLK), (1, 0, 2))

    def hidden_block(operands):
        gate_w, up_w, gate_l, up_l = operands
        gate_sum = listed_sum(feature_blocks, gate_w, gate_l)
        up_sum = listed_sum(feature_blocks, up_w, up_l)
        return (jax.nn.silu(gate_sum) * up_sum).astype(jnp.bfloat16)

    hidden = lax.map(hidden_block, (gate_weight, up_weight, gate_list, up_list))

    def output_block(operands):
        down_w, down_l = operands
        return listed_sum(hidden, down_w, down_l).astype(jnp.bfloat16)

    mixed_out = lax.map(output_block, (down_weight, down_list))
    return jnp.transpose(mixed_out, (1, 0, 2)).reshape(TOKENS, ROWB * BLK)
```

```python
import functools

import jax
import jax.numpy as jnp
from jax import lax
from jax.experimental import pallas as pl
from jax.experimental.pallas import tpu as pltpu
from jax.sharding import PartitionSpec as P

MESH = pl.DeviceIdType.MESH


def exchange_kernel(
    sizes, ids_ref, rows_ref, tok_ref, gate_ref, up_ref, down_ref,
    feat_ref, got_ref, down_out, rows_out,
    sel, zero, zr_s, zr_r, zl_s, zl_r, y_s, y_r, wx_s, wx_r, li_s, li_r, xs_s, xs_r, sib_s, sib_r, loc,
):
    nt, nw, cap = sizes
    xs, ys = nt // 2, nt // 2
    zs = nw // ys
    t, w = lax.axis_index("tok"), lax.axis_index("wa")
    x, c = lax.div(t, 2), lax.rem(t, 2)
    z, y = lax.div(w, ys), lax.rem(w, ys)
    fb = tok_ref.shape[0]

    barrier = pltpu.get_barrier_semaphore()
    for r in range(1, nw):
        pl.semaphore_signal(barrier, inc=1, device_id=(t, lax.rem(w + r, nw)), device_id_type=MESH)
    for r in range(1, nt):
        pl.semaphore_signal(barrier, inc=1, device_id=(lax.rem(t + r, nt), w), device_id_type=MESH)
    pl.semaphore_wait(barrier, nw + nt - 2)

    def remote(src, dst, ssem, rsem, dev):
        return pltpu.make_async_remote_copy(
            src_ref=src, dst_ref=dst, send_sem=ssem, recv_sem=rsem, device_id=dev, device_id_type=MESH
        )

    def feat(src):
        return feat_ref.at[pl.ds(src * fb, fb)]

    def right(k, src):
        return remote(src, feat(w - (k - 1) * ys), zr_s.at[k - 1], zr_r.at[k - 1], (t, w + ys))

    def left(k, src):
        return remote(src, feat(w + (k - 1) * ys), zl_s.at[k - 1], zl_r.at[k - 1], (t, w - ys))

    def across(zz, dy, src):
        return remote(
            src, feat(zz * ys + y), y_s.at[zz, dy - 1], y_r.at[zz, dy - 1], (t, z * ys + lax.rem(y + dy, ys))
        )

    def send_right(k, src):
        pl.when((z + 1 < zs) & (z - (k - 1) >= 0))(lambda: right(k, src).start())

    def send_left(k, src):
        pl.when((z >= 1) & (z + (k - 1) < zs))(lambda: left(k, src).start())

    send_right(1, tok_ref)
    send_left(1, tok_ref)
    for dy in range(1, ys):
        across(z, dy, tok_ref).start()

    def sibling(j, e, src, dst):
        return remote(src, dst, sib_s.at[j, e], sib_r.at[j, e], (x * 2 + (1 - c), w))

    def along_x(j, dx, src, dst):
        return remote(src, dst, xs_s.at[j, dx - 1], xs_r.at[j, dx - 1], (lax.rem(x + dx, xs) * 2 + c, w))

    def source(j):
        return lax.rem(w + nw - j, nw)

    def slot(j, tt):
        return down_out.at[tt] if j == nw else got_ref.at[tt, source(j)]

    def from_x(dx):
        return lax.rem(x + xs - dx, xs) * 2 + c

    def spread(j, src):
        for dx in range(1, xs):
            along_x(j, dx, src, slot(j, t)).start()
        sibling(j, 0, src, slot(j, t)).start()

    spread(nw, down_ref)

    zero[...] = jnp.zeros_like(zero)
    own_copies = [
        pltpu.make_async_copy(zero, feat_ref.at[nw * fb], loc.at[0]),
        pltpu.make_async_copy(tok_ref, feat(w), loc.at[1]),
        pltpu.make_async_copy(down_ref, down_out.at[t], loc.at[2]),
        pltpu.make_async_copy(sel.at[w], got_ref.at[t, w], loc.at[3]),
        pltpu.make_async_copy(rows_ref.at[w], rows_out.at[w], loc.at[4]),
    ]
    for copy in own_copies[:3]:
        copy.start()

    def pick(d):
        for s in range(cap):
            chosen = ids_ref[d * cap + s]
            sel[d, s, 0] = gate_ref[chosen]
            sel[d, s, 1] = up_ref[chosen]

    pick(w)
    own_copies[3].start()
    own_copies[4].start()
    spread(0, sel.at[w])

    def to_dest(r):
        return remote(
            sel.at[lax.rem(w + r, nw)], got_ref.at[t, w], wx_s.at[r - 1], wx_r.at[r - 1], (t, lax.rem(w + r, nw))
        )

    def rows_to_dest(r):
        return remote(
            rows_ref.at[lax.rem(w + r, nw)], rows_out.at[w], li_s.at[r - 1], li_r.at[r - 1], (t, lax.rem(w + r, nw))
        )

    for r in range(1, nw):
        pick(lax.rem(w + r, nw))
        to_dest(r).start()
        rows_to_dest(r).start()

    def forward_tokens(k):
        @pl.when(z - k >= 0)
        def _():
            block = feat(w - k * ys)
            remote(block, block, zr_s.at[k - 1], zr_r.at[k - 1], (t, w)).wait_recv()
            if k < zs - 1:
                send_right(k + 1, block)
            for dy in range(1, ys):
                across(z - k, dy, block).start()

        @pl.when(z + k < zs)
        def _():
            block = feat(w + k * ys)
            remote(block, block, zl_s.at[k - 1], zl_r.at[k - 1], (t, w)).wait_recv()
            if k < zs - 1:
                send_left(k + 1, block)
            for dy in range(1, ys):
                across(z + k, dy, block).start()

    def forward_weights(j):
        to_me = got_ref.at[t, source(j)]
        remote(to_me, to_me, wx_s.at[j - 1], wx_r.at[j - 1], (t, w)).wait_recv()
        spread(j, to_me)

    def forward_sibling(j):
        for dx in range(1, xs):
            there = slot(j, from_x(dx))
            along_x(j, dx, there, there).wait_recv()
            sibling(j, dx, there, there).start()

    forward_sibling(nw)
    per = -(-(nw - 1) // (zs - 1))
    for k in range(1, zs):
        forward_tokens(k)
        for j in range((k - 1) * per + 1, min(k * per, nw - 1) + 1):
            forward_weights(j)
            forward_sibling(j - 1)
    forward_sibling(nw - 1)

    for zz in range(zs):
        for dy in range(1, ys):
            block = feat(zz * ys + lax.rem(y + ys - dy, ys))
            across(zz, dy, block).wait_recv()
    for r in range(1, nw):
        row = rows_out.at[source(r)]
        remote(row, row, li_s.at[r - 1], li_r.at[r - 1], (t, w)).wait_recv()
    for j in [*range(nw), nw]:
        other = x * 2 + (1 - c)
        sibling(j, 0, slot(j, other), slot(j, other)).wait_recv()
        for dx in range(1, xs):
            there = slot(j, lax.rem(x + xs - dx, xs) * 2 + (1 - c))
            sibling(j, dx, there, there).wait_recv()
    for copy in own_copies:
        copy.wait()
    for k in range(1, zs):
        pl.when((z + 1 < zs) & (z - (k - 1) >= 0))(lambda: right(k, tok_ref).wait_send())
        pl.when((z >= 1) & (z + (k - 1) < zs))(lambda: left(k, tok_ref).wait_send())
    for zz in range(zs):
        for dy in range(1, ys):
            across(zz, dy, tok_ref).wait_send()
    for r in range(1, nw):
        to_dest(r).wait_send()
        rows_to_dest(r).wait_send()
    for j in [*range(nw), nw]:
        for dx in range(1, xs):
            along_x(j, dx, slot(j, t), slot(j, t)).wait_send()
        for e in range(xs):
            sibling(j, e, slot(j, t), slot(j, t)).wait_send()


def exchange(sizes, ids, rows, tokens, gate, up, down):
    nt, nw, cap = sizes
    fb, row_count, blk = tokens.shape
    slots = gate.shape[1]
    xs = ys = nt // 2
    zs = nw // ys
    sem = pltpu.SemaphoreType.DMA
    dtype = tokens.dtype
    any_spec = pl.BlockSpec(memory_space=pl.ANY)
    vmem_spec = pl.BlockSpec(memory_space=pltpu.VMEM)
    return pl.pallas_call(
        functools.partial(exchange_kernel, sizes),
        out_shape=(
            jax.ShapeDtypeStruct((nw * fb + 1, row_count, blk), dtype),
            jax.ShapeDtypeStruct((nt, nw, cap, 2, slots, blk, blk), dtype),
            jax.ShapeDtypeStruct((nt, *down.shape), dtype),
            jax.ShapeDtypeStruct(rows.shape, rows.dtype),
        ),
        in_specs=[pl.BlockSpec(memory_space=pltpu.SMEM), any_spec, any_spec, vmem_spec, vmem_spec, any_spec],
        out_specs=(any_spec,) * 4,
        scratch_shapes=[
            pltpu.VMEM((nw, cap, 2, slots, blk, blk), dtype),
            pltpu.VMEM((row_count, blk), dtype),
            sem((zs - 1,)), sem((zs - 1,)), sem((zs - 1,)), sem((zs - 1,)),
            sem((zs, ys - 1)), sem((zs, ys - 1)),
            sem((nw - 1,)), sem((nw - 1,)), sem((nw - 1,)), sem((nw - 1,)),
            sem((nw + 1, xs - 1)), sem((nw + 1, xs - 1)), sem((nw + 1, xs)), sem((nw + 1, xs)),
            sem((5,)),
        ],
        compiler_params=pltpu.CompilerParams(
            collective_id=0, has_side_effects=True, vmem_limit_bytes=24 << 20
        ),
    )(ids, rows, tokens, gate, up, down)


def layer_kernel(sizes, rows_ref, places_ref, feat_ref, got_ref, down_ref, out_ref, hidden):
    nt, nw, cap, kg, kd, none = sizes
    step = pl.program_id(0)
    blk = feat_ref.shape[2]

    def column(s, which):
        base = ((step * cap + s) * 2 + which) * kg
        lhs = jnp.concatenate([feat_ref[rows_ref[base + k]] for k in range(kg)], axis=1)
        rhs = jnp.concatenate([got_ref[tt, 0, s, which].reshape(-1, blk) for tt in range(nt)], axis=0)
        return jnp.dot(lhs, rhs, preferred_element_type=jnp.float32)

    @pl.when(step == 0)
    def _():
        hidden[nw * cap] = jnp.zeros(hidden.shape[1:], hidden.dtype)

    for s in range(cap):
        gate = column(s, 0)
        up = column(s, 1)
        hidden[step * cap + s] = (gate / (1.0 + jnp.exp(-gate)) * up).astype(hidden.dtype)

    @pl.when(step == nw - 1)
    def _():
        for b in range(out_ref.shape[1] // blk):
            lhs = jnp.concatenate([hidden[places_ref[b * kd + k]] for k in range(kd)], axis=1)
            rhs = jnp.concatenate([down_ref[tt, b].reshape(-1, blk) for tt in range(nt)], axis=0)
            out_ref[:, b * blk : (b + 1) * blk] = jnp.dot(
                lhs, rhs, preferred_element_type=jnp.float32
            ).astype(out_ref.dtype)


def layer(sizes, rows, places, feat, got, down):
    nt, nw, cap, kg, kd, none = sizes
    row_count, blk = feat.shape[1:]
    outs = down.shape[1]
    vmem_spec = pl.BlockSpec(memory_space=pltpu.VMEM)
    return pl.pallas_call(
        functools.partial(layer_kernel, sizes),
        out_shape=jax.ShapeDtypeStruct((row_count, outs * blk), feat.dtype),
        grid_spec=pltpu.PrefetchScalarGridSpec(
            num_scalar_prefetch=2,
            grid=(nw,),
            in_specs=[
                vmem_spec,
                pl.BlockSpec((nt, 1, *got.shape[2:]), lambda i, a, b: (0, i, 0, 0, 0, 0, 0)),
                vmem_spec,
            ],
            out_specs=pl.BlockSpec((row_count, outs * blk), lambda i, a, b: (0, 0)),
            scratch_shapes=[pltpu.VMEM((nw * cap + 1, row_count, blk), feat.dtype)],
        ),
        compiler_params=pltpu.CompilerParams(vmem_limit_bytes=48 << 20),
    )(rows, places, feat, got, down)


def running(flags):
    upto = jnp.arange(flags.shape[1])
    upto = upto[:, None] >= upto[None, :]
    return jnp.sum((flags[:, None, :] & upto[None]).astype(jnp.int32), axis=2)


def on_device(tokens, gate_weight, up_weight, down_weight, gate_list, up_list, down_list):
    nt, nw = lax.axis_size("tok"), lax.axis_size("wa")
    me = lax.axis_index("wa")
    hid_blocks, _, blk, _ = gate_weight.shape
    outs = down_weight.shape[0]
    kd, kg = down_list.shape[1], gate_list.shape[1]
    cap = max(2, (kd + nw - 1) // nw + 1)
    row_count = tokens.shape[0]
    fb = tokens.shape[1] // blk
    groups = down_list.reshape(nw, -1)

    own_ids = me * hid_blocks + jnp.arange(hid_blocks, dtype=jnp.int32)
    wanted = jnp.any(groups[:, :, None] == own_ids[None, None, :], axis=1)
    places = running(wanted) - 1
    chosen = wanted[:, None, :] & (places[:, None, :] == jnp.arange(cap, dtype=jnp.int32)[None, :, None])
    ids = jnp.sum(jnp.where(chosen, jnp.arange(hid_blocks, dtype=jnp.int32), 0), axis=2)
    both = jnp.concatenate([gate_list, up_list], axis=1)
    both = jnp.where(both < 0, nw * fb, both)
    picked = jnp.sum(jnp.where(chosen[..., None], both[None, None], 0), axis=2).reshape(nw, -1)
    width = -(-picked.shape[1] // 1024) * 1024
    rows = jnp.pad(picked, ((0, 0), (0, width - picked.shape[1]))).reshape(nw, -1, 128)

    mine = lax.dynamic_slice_in_dim(down_list, me * outs, outs, 0)
    all_ids = jnp.arange(nw * hid_blocks, dtype=jnp.int32)
    hit = mine.reshape(-1)[:, None] == all_ids[None, :]
    named = jnp.any(hit, axis=0).reshape(nw, hid_blocks)
    spot = running(named) - 1 + cap * jnp.arange(nw, dtype=jnp.int32)[:, None]
    spots = jnp.sum(jnp.where(hit, spot.reshape(1, -1), 0), axis=1)
    spots = jnp.where(mine.reshape(-1) >= 0, spots, nw * cap)

    blocks = jnp.transpose(tokens.reshape(row_count, fb, blk), (1, 0, 2))
    feat, got, down, got_rows = exchange(
        (nt, nw, cap), ids.reshape(-1), rows, blocks, gate_weight, up_weight, down_weight
    )
    lists = got_rows.reshape(nw, -1)[:, : cap * 2 * kg].reshape(-1)
    return layer((nt, nw, cap, kg, kd, nw * fb), lists, spots, feat, got, down)


def solution(mesh):
    placed = (
        P("tok", "wa"),
        P("wa", "tok", None, None),
        P("wa", "tok", None, None),
        P("wa", "tok", None, None),
        P("wa", None),
        P("wa", None),
        P(),
    )
    return jax.shard_map(
        on_device, mesh=mesh, in_specs=placed, out_specs=P("tok", "wa"), check_vma=False
    )
```

```python
import functools

import jax
import jax.numpy as jnp
from jax import lax
from jax.experimental import pallas as pl
from jax.experimental.pallas import tpu as pltpu
from jax.sharding import PartitionSpec as P

MESH = pl.DeviceIdType.MESH
FIRST = 2
EARLY = 3


def layer_kernel(
    sizes, ids_ref, spots_ref, rows_ref, tok_ref, gate_hbm, up_hbm, down_ref, out_ref,
    feat_ref, got_ref, down_out, rows_out, lists, hidden, gate_ref, up_ref,
    sel, zr_s, zr_r, zl_s, zl_r, y_s, y_r, wx_s, wx_r, li_s, li_r, xs_s, xs_r, sib_s, sib_r, loc,
):
    nt, nw, cap, kg, kd = sizes
    xs, ys = nt // 2, nt // 2
    zs = nw // ys
    t, w = lax.axis_index("tok"), lax.axis_index("wa")
    x, c = lax.div(t, 2), lax.rem(t, 2)
    z, y = lax.div(w, ys), lax.rem(w, ys)
    fb, row_count, blk = tok_ref.shape
    loads = [
        pltpu.make_async_copy(gate_hbm, gate_ref, loc.at[0]),
        pltpu.make_async_copy(up_hbm, up_ref, loc.at[1]),
    ]
    for copy in loads:
        copy.start()

    barrier = pltpu.get_barrier_semaphore()
    for r in range(1, nw):
        pl.semaphore_signal(barrier, inc=1, device_id=(t, lax.rem(w + r, nw)), device_id_type=MESH)
    for r in range(1, nt):
        pl.semaphore_signal(barrier, inc=1, device_id=(lax.rem(t + r, nt), w), device_id_type=MESH)
    pl.semaphore_wait(barrier, nw + nt - 2)

    def remote(src, dst, ssem, rsem, dev):
        return pltpu.make_async_remote_copy(
            src_ref=src, dst_ref=dst, send_sem=ssem, recv_sem=rsem, device_id=dev, device_id_type=MESH
        )

    def feat(src):
        return feat_ref.at[pl.ds(src * fb, fb)]

    def right(k, src):
        return remote(src, feat(w - (k - 1) * ys), zr_s.at[k - 1], zr_r.at[k - 1], (t, w + ys))

    def left(k, src):
        return remote(src, feat(w + (k - 1) * ys), zl_s.at[k - 1], zl_r.at[k - 1], (t, w - ys))

    def across(zz, dy, src):
        return remote(
            src, feat(zz * ys + y), y_s.at[zz, dy - 1], y_r.at[zz, dy - 1], (t, z * ys + lax.rem(y + dy, ys))
        )

    def send_right(k, src):
        pl.when((z + 1 < zs) & (z - (k - 1) >= 0))(lambda: right(k, src).start())

    def send_left(k, src):
        pl.when((z >= 1) & (z + (k - 1) < zs))(lambda: left(k, src).start())

    send_right(1, tok_ref)
    send_left(1, tok_ref)
    for dy in range(1, ys):
        across(z, dy, tok_ref).start()

    def sibling(j, e, src, dst):
        return remote(src, dst, sib_s.at[j, e], sib_r.at[j, e], (x * 2 + (1 - c), w))

    def along_x(j, dx, src, dst):
        return remote(src, dst, xs_s.at[j, dx - 1], xs_r.at[j, dx - 1], (lax.rem(x + dx, xs) * 2 + c, w))

    def source(j):
        return lax.rem(w + nw - j, nw)

    def slot(j, tt):
        return got_ref.at[tt, source(j)]

    def down_slot(j, tt):
        return down_out.at[tt]

    def from_x(dx, core):
        return lax.rem(x + xs - dx, xs) * 2 + core

    def spread(j, src, at=slot):
        for dx in range(1, xs):
            along_x(j, dx, src, at(j, t)).start()
        sibling(j, 0, src, at(j, t)).start()

    spread(nw, down_ref, down_slot)

    def pick(d):
        for s in range(cap):
            chosen = ids_ref[d * cap + s]
            sel[d, s, 0] = gate_ref[chosen]
            sel[d, s, 1] = up_ref[chosen]

    for copy in loads:
        copy.wait()
    pick(w)
    spread(0, sel.at[w])
    own_copies = [
        pltpu.make_async_copy(tok_ref, feat(w), loc.at[2]),
        pltpu.make_async_copy(down_ref, down_out.at[t], loc.at[3]),
        pltpu.make_async_copy(sel.at[w], got_ref.at[t, w], loc.at[4]),
        pltpu.make_async_copy(rows_ref.at[w], rows_out.at[w], loc.at[5]),
    ]
    for copy in own_copies:
        copy.start()

    def to_dest(r):
        d = lax.rem(w + r, nw)
        return remote(sel.at[d], got_ref.at[t, w], wx_s.at[r - 1], wx_r.at[r - 1], (t, d))

    def rows_to_dest(r):
        d = lax.rem(w + r, nw)
        return remote(rows_ref.at[d], rows_out.at[w], li_s.at[r - 1], li_r.at[r - 1], (t, d))

    @pl.loop(1, nw)
    def _(r):
        rows_to_dest(r).start()
        pick(lax.rem(w + r, nw))

    feat_ref[nw * fb] = jnp.zeros((row_count, blk), feat_ref.dtype)
    hidden[nw * cap] = jnp.zeros((row_count, blk), hidden.dtype)

    first = -(-(nw - 1) * FIRST // 8)
    per = -(-(nw - 1 - first) // (zs - 1))

    def batch(lo, hi):
        for r in range(lo, min(hi, nw)):
            to_dest(r).start()

    batch(1, 1 + first)

    def forward_tokens(k):
        @pl.when(z - k >= 0)
        def _():
            block = feat(w - k * ys)
            remote(block, block, zr_s.at[k - 1], zr_r.at[k - 1], (t, w)).wait_recv()
            if k < zs - 1:
                send_right(k + 1, block)
            for dy in range(1, ys):
                across(z - k, dy, block).start()

        @pl.when(z + k < zs)
        def _():
            block = feat(w + k * ys)
            remote(block, block, zl_s.at[k - 1], zl_r.at[k - 1], (t, w)).wait_recv()
            if k < zs - 1:
                send_left(k + 1, block)
            for dy in range(1, ys):
                across(z + k, dy, block).start()

    def forward_weights(j):
        to_me = slot(j, t)
        remote(to_me, to_me, wx_s.at[j - 1], wx_r.at[j - 1], (t, w)).wait_recv()
        spread(j, to_me)

    def forward_sibling(j, at=slot):
        for dx in range(1, xs):
            there = at(j, from_x(dx, c))
            along_x(j, dx, there, there).wait_recv()
            sibling(j, dx, there, there).start()

    def wait_sibling(j, at=slot):
        for e in range(xs):
            there = at(j, from_x(e, 1 - c))
            sibling(j, e, there, there).wait_recv()

    for k in range(1, zs):
        forward_tokens(k)
        batch(1 + first + (k - 1) * per, 1 + first + k * per)
    early = min(EARLY, nw - 1)
    for j in range(1, early + 1):
        forward_weights(j)
    forward_sibling(nw, down_slot)
    forward_sibling(0)
    for copy in own_copies:
        copy.wait()
    for zz in range(zs):
        for dy in range(1, ys):
            block = feat(zz * ys + lax.rem(y + ys - dy, ys))
            across(zz, dy, block).wait_recv()

    @pl.loop(1, nw)
    def _(r):
        row = rows_out.at[source(r)]
        remote(row, row, li_s.at[r - 1], li_r.at[r - 1], (t, w)).wait_recv()

    to_scalars = pltpu.make_async_copy(rows_out, lists, loc.at[6])
    to_scalars.start()
    to_scalars.wait()

    def column(origin, s, which):
        base = (s * 2 + which) * kg
        picks = [feat_ref[lists[origin, (base + k) // 128, (base + k) % 128]] for k in range(kg)]
        rhs = [got_ref[tt, origin, s, which].reshape(-1, blk) for tt in range(nt)]
        return jnp.dot(
            jnp.concatenate(picks, axis=1), jnp.concatenate(rhs, axis=0), preferred_element_type=jnp.float32
        )

    @pl.loop(0, nw)
    def _(i):
        pl.when(i + early + 1 < nw)(lambda: forward_weights(i + early + 1))
        pl.when(i + 1 < nw)(lambda: forward_sibling(i + 1))
        wait_sibling(i)
        origin = source(i)
        for s in range(cap):
            gate = column(origin, s, 0)
            up = column(origin, s, 1)
            hidden[origin * cap + s] = (gate / (1.0 + jnp.exp(-gate)) * up).astype(hidden.dtype)

    wait_sibling(nw, down_slot)
    for b in range(down_ref.shape[0]):
        lhs = jnp.concatenate([hidden[spots_ref[b * kd + k]] for k in range(kd)], axis=1)
        rhs = jnp.concatenate([down_out[tt, b].reshape(-1, blk) for tt in range(nt)], axis=0)
        out_ref[:, b * blk : (b + 1) * blk] = jnp.dot(lhs, rhs, preferred_element_type=jnp.float32).astype(
            out_ref.dtype
        )

    for k in range(1, zs):
        pl.when((z + 1 < zs) & (z - (k - 1) >= 0))(lambda: right(k, tok_ref).wait_send())
        pl.when((z >= 1) & (z + (k - 1) < zs))(lambda: left(k, tok_ref).wait_send())
    for zz in range(zs):
        for dy in range(1, ys):
            across(zz, dy, tok_ref).wait_send()

    @pl.loop(1, nw)
    def _(r):
        to_dest(r).wait_send()
        rows_to_dest(r).wait_send()

    def sent(j, at=slot):
        for dx in range(1, xs):
            along_x(j, dx, at(j, t), at(j, t)).wait_send()
        for e in range(xs):
            sibling(j, e, at(j, t), at(j, t)).wait_send()

    pl.loop(0, nw)(sent)
    sent(nw, down_slot)


def layer(sizes, ids, spots, rows, tokens, gate, up, down):
    nt, nw, cap, kg, kd = sizes
    fb, row_count, blk = tokens.shape
    slots, outs = gate.shape[1], down.shape[0]
    xs = ys = nt // 2
    zs = nw // ys
    sem = pltpu.SemaphoreType.DMA
    dtype = tokens.dtype
    any_spec = pl.BlockSpec(memory_space=pl.ANY)
    vmem_spec = pl.BlockSpec(memory_space=pltpu.VMEM)
    smem_spec = pl.BlockSpec(memory_space=pltpu.SMEM)
    return pl.pallas_call(
        functools.partial(layer_kernel, sizes),
        out_shape=jax.ShapeDtypeStruct((row_count, outs * blk), dtype),
        in_specs=[smem_spec, smem_spec, vmem_spec, any_spec, any_spec, any_spec, any_spec],
        out_specs=vmem_spec,
        scratch_shapes=[
            pltpu.VMEM((nw * fb + 1, row_count, blk), dtype),
            pltpu.VMEM((nt, nw, cap, 2, slots, blk, blk), dtype),
            pltpu.VMEM((nt, *down.shape), dtype),
            pltpu.VMEM(rows.shape, rows.dtype),
            pltpu.SMEM(rows.shape, rows.dtype),
            pltpu.VMEM((nw * cap + 1, row_count, blk), dtype),
            pltpu.VMEM(gate.shape, dtype),
            pltpu.VMEM(up.shape, dtype),
            pltpu.VMEM((nw, cap, 2, slots, blk, blk), dtype),
            sem((zs - 1,)), sem((zs - 1,)), sem((zs - 1,)), sem((zs - 1,)),
            sem((zs, ys - 1)), sem((zs, ys - 1)),
            sem((nw - 1,)), sem((nw - 1,)), sem((nw - 1,)), sem((nw - 1,)),
            sem((nw + 1, xs - 1)), sem((nw + 1, xs - 1)), sem((nw + 1, xs)), sem((nw + 1, xs)),
            sem((7,)),
        ],
        compiler_params=pltpu.CompilerParams(
            collective_id=0, has_side_effects=True, vmem_limit_bytes=60 << 20
        ),
    )(ids, spots, rows, tokens, gate, up, down)


def running(flags):
    upto = jnp.arange(flags.shape[1])
    upto = upto[:, None] >= upto[None, :]
    return jnp.sum((flags[:, None, :] & upto[None]).astype(jnp.int32), axis=2)


def on_device(tokens, gate_weight, up_weight, down_weight, gate_list, up_list, down_list):
    nt, nw = lax.axis_size("tok"), lax.axis_size("wa")
    me = lax.axis_index("wa")
    hid_blocks, _, blk, _ = gate_weight.shape
    outs = down_weight.shape[0]
    kd, kg = down_list.shape[1], gate_list.shape[1]
    cap = max(2, (kd + nw - 1) // nw + 1)
    row_count = tokens.shape[0]
    fb = tokens.shape[1] // blk
    groups = down_list.reshape(nw, -1)

    own_ids = me * hid_blocks + jnp.arange(hid_blocks, dtype=jnp.int32)
    wanted = jnp.any(groups[:, :, None] == own_ids[None, None, :], axis=1)
    places = running(wanted) - 1
    chosen = wanted[:, None, :] & (places[:, None, :] == jnp.arange(cap, dtype=jnp.int32)[None, :, None])
    ids = jnp.sum(jnp.where(chosen, jnp.arange(hid_blocks, dtype=jnp.int32), 0), axis=2)
    both = jnp.concatenate([gate_list, up_list], axis=1)
    both = jnp.where(both < 0, nw * fb, both)
    picked = jnp.sum(jnp.where(chosen[..., None], both[None, None], 0), axis=2).reshape(nw, -1)
    width = -(-picked.shape[1] // 1024) * 1024
    rows = jnp.pad(picked, ((0, 0), (0, width - picked.shape[1]))).reshape(nw, -1, 128)

    mine = lax.dynamic_slice_in_dim(down_list, me * outs, outs, 0)
    all_ids = jnp.arange(nw * hid_blocks, dtype=jnp.int32)
    hit = mine.reshape(-1)[:, None] == all_ids[None, :]
    named = jnp.any(hit, axis=0).reshape(nw, hid_blocks)
    spot = running(named) - 1 + cap * jnp.arange(nw, dtype=jnp.int32)[:, None]
    spots = jnp.sum(jnp.where(hit, spot.reshape(1, -1), 0), axis=1)
    spots = jnp.where(mine.reshape(-1) >= 0, spots, nw * cap)

    blocks = jnp.transpose(tokens.reshape(row_count, fb, blk), (1, 0, 2))
    return layer(
        (nt, nw, cap, kg, kd), ids.reshape(-1), spots, rows, blocks, gate_weight, up_weight, down_weight
    )


def solution(mesh):
    placed = (
        P("tok", "wa"),
        P("wa", "tok", None, None),
        P("wa", "tok", None, None),
        P("wa", "tok", None, None),
        P("wa", None),
        P("wa", None),
        P(),
    )
    return jax.shard_map(
        on_device, mesh=mesh, in_specs=placed, out_specs=P("tok", "wa"), check_vma=False
    )
```

```python
import functools

import jax
import jax.numpy as jnp
from jax import lax
from jax.experimental import pallas as pl
from jax.experimental.pallas import tpu as pltpu
from jax.sharding import PartitionSpec as P

MESH = pl.DeviceIdType.MESH


def exchange_kernel(
    sizes, ids_ref, rows_ref, tok_ref, gate_hbm, up_hbm, down_ref,
    feat_ref, got_ref, down_out, rows_out,
    gate_ref, up_ref, sel, zero, zr_s, zr_r, zl_s, zl_r, y_s, y_r, wx_s, wx_r, li_s, li_r, xs_s, xs_r, sib_s, sib_r, loc,
):
    nt, nw, cap = sizes
    xs, ys = nt // 2, nt // 2
    zs = nw // ys
    t, w = lax.axis_index("tok"), lax.axis_index("wa")
    x, c = lax.div(t, 2), lax.rem(t, 2)
    z, y = lax.div(w, ys), lax.rem(w, ys)
    fb = tok_ref.shape[0]
    loads = [
        pltpu.make_async_copy(gate_hbm, gate_ref, loc.at[5]),
        pltpu.make_async_copy(up_hbm, up_ref, loc.at[6]),
    ]
    for copy in loads:
        copy.start()

    barrier = pltpu.get_barrier_semaphore()
    for r in range(1, nw):
        pl.semaphore_signal(barrier, inc=1, device_id=(t, lax.rem(w + r, nw)), device_id_type=MESH)
    for r in range(1, nt):
        pl.semaphore_signal(barrier, inc=1, device_id=(lax.rem(t + r, nt), w), device_id_type=MESH)
    pl.semaphore_wait(barrier, nw + nt - 2)

    def remote(src, dst, ssem, rsem, dev):
        return pltpu.make_async_remote_copy(
            src_ref=src, dst_ref=dst, send_sem=ssem, recv_sem=rsem, device_id=dev, device_id_type=MESH
        )

    def feat(src):
        return feat_ref.at[pl.ds(src * fb, fb)]

    def right(k, src):
        return remote(src, feat(w - (k - 1) * ys), zr_s.at[k - 1], zr_r.at[k - 1], (t, w + ys))

    def left(k, src):
        return remote(src, feat(w + (k - 1) * ys), zl_s.at[k - 1], zl_r.at[k - 1], (t, w - ys))

    def across(zz, dy, src):
        return remote(
            src, feat(zz * ys + y), y_s.at[zz, dy - 1], y_r.at[zz, dy - 1], (t, z * ys + lax.rem(y + dy, ys))
        )

    def send_right(k, src):
        pl.when((z + 1 < zs) & (z - (k - 1) >= 0))(lambda: right(k, src).start())

    def send_left(k, src):
        pl.when((z >= 1) & (z + (k - 1) < zs))(lambda: left(k, src).start())

    send_right(1, tok_ref)
    send_left(1, tok_ref)
    for dy in range(1, ys):
        across(z, dy, tok_ref).start()

    def sibling(j, e, src, dst):
        return remote(src, dst, sib_s.at[j, e], sib_r.at[j, e], (x * 2 + (1 - c), w))

    def along_x(j, dx, src, dst):
        return remote(src, dst, xs_s.at[j, dx - 1], xs_r.at[j, dx - 1], (lax.rem(x + dx, xs) * 2 + c, w))

    def source(j):
        return lax.rem(w + nw - j, nw)

    def slot(j, tt):
        return down_out.at[tt] if j == nw else got_ref.at[tt, source(j)]

    def from_x(dx):
        return lax.rem(x + xs - dx, xs) * 2 + c

    def spread(j, src):
        for dx in range(1, xs):
            along_x(j, dx, src, slot(j, t)).start()
        sibling(j, 0, src, slot(j, t)).start()

    spread(nw, down_ref)

    zero[...] = jnp.zeros_like(zero)
    own_copies = [
        pltpu.make_async_copy(zero, feat_ref.at[nw * fb], loc.at[0]),
        pltpu.make_async_copy(tok_ref, feat(w), loc.at[1]),
        pltpu.make_async_copy(down_ref, down_out.at[t], loc.at[2]),
        pltpu.make_async_copy(sel.at[w], got_ref.at[t, w], loc.at[3]),
        pltpu.make_async_copy(rows_ref.at[w], rows_out.at[w], loc.at[4]),
    ]
    for copy in own_copies[:3]:
        copy.start()

    def pick(d):
        for s in range(cap):
            chosen = ids_ref[d * cap + s]
            sel[d, s, 0] = gate_ref[chosen]
            sel[d, s, 1] = up_ref[chosen]

    for copy in loads:
        copy.wait()
    pick(w)
    own_copies[3].start()
    own_copies[4].start()
    spread(0, sel.at[w])

    def to_dest(r):
        return remote(
            sel.at[lax.rem(w + r, nw)], got_ref.at[t, w], wx_s.at[r - 1], wx_r.at[r - 1], (t, lax.rem(w + r, nw))
        )

    def rows_to_dest(r):
        return remote(
            rows_ref.at[lax.rem(w + r, nw)], rows_out.at[w], li_s.at[r - 1], li_r.at[r - 1], (t, lax.rem(w + r, nw))
        )

    for r in range(1, nw):
        pick(lax.rem(w + r, nw))
        to_dest(r).start()
        rows_to_dest(r).start()

    def forward_tokens(k):
        @pl.when(z - k >= 0)
        def _():
            block = feat(w - k * ys)
            remote(block, block, zr_s.at[k - 1], zr_r.at[k - 1], (t, w)).wait_recv()
            if k < zs - 1:
                send_right(k + 1, block)
            for dy in range(1, ys):
                across(z - k, dy, block).start()

        @pl.when(z + k < zs)
        def _():
            block = feat(w + k * ys)
            remote(block, block, zl_s.at[k - 1], zl_r.at[k - 1], (t, w)).wait_recv()
            if k < zs - 1:
                send_left(k + 1, block)
            for dy in range(1, ys):
                across(z + k, dy, block).start()

    def forward_weights(j):
        to_me = got_ref.at[t, source(j)]
        remote(to_me, to_me, wx_s.at[j - 1], wx_r.at[j - 1], (t, w)).wait_recv()
        spread(j, to_me)

    def forward_sibling(j):
        for dx in range(1, xs):
            there = slot(j, from_x(dx))
            along_x(j, dx, there, there).wait_recv()
            sibling(j, dx, there, there).start()

    forward_sibling(nw)
    per = -(-(nw - 1) // (zs - 1))
    for k in range(1, zs):
        forward_tokens(k)
        for j in range((k - 1) * per + 1, min(k * per, nw - 1) + 1):
            forward_weights(j)
            forward_sibling(j - 1)
    forward_sibling(nw - 1)

    for zz in range(zs):
        for dy in range(1, ys):
            block = feat(zz * ys + lax.rem(y + ys - dy, ys))
            across(zz, dy, block).wait_recv()
    for r in range(1, nw):
        row = rows_out.at[source(r)]
        remote(row, row, li_s.at[r - 1], li_r.at[r - 1], (t, w)).wait_recv()
    for j in [*range(nw), nw]:
        other = x * 2 + (1 - c)
        sibling(j, 0, slot(j, other), slot(j, other)).wait_recv()
        for dx in range(1, xs):
            there = slot(j, lax.rem(x + xs - dx, xs) * 2 + (1 - c))
            sibling(j, dx, there, there).wait_recv()
    for copy in own_copies:
        copy.wait()
    for k in range(1, zs):
        pl.when((z + 1 < zs) & (z - (k - 1) >= 0))(lambda: right(k, tok_ref).wait_send())
        pl.when((z >= 1) & (z + (k - 1) < zs))(lambda: left(k, tok_ref).wait_send())
    for zz in range(zs):
        for dy in range(1, ys):
            across(zz, dy, tok_ref).wait_send()
    for r in range(1, nw):
        to_dest(r).wait_send()
        rows_to_dest(r).wait_send()
    for j in [*range(nw), nw]:
        for dx in range(1, xs):
            along_x(j, dx, slot(j, t), slot(j, t)).wait_send()
        for e in range(xs):
            sibling(j, e, slot(j, t), slot(j, t)).wait_send()


def exchange(sizes, ids, rows, tokens, gate, up, down):
    nt, nw, cap = sizes
    fb, row_count, blk = tokens.shape
    slots = gate.shape[1]
    xs = ys = nt // 2
    zs = nw // ys
    sem = pltpu.SemaphoreType.DMA
    dtype = tokens.dtype
    any_spec = pl.BlockSpec(memory_space=pl.ANY)
    return pl.pallas_call(
        functools.partial(exchange_kernel, sizes),
        out_shape=(
            jax.ShapeDtypeStruct((nw * fb + 1, row_count, blk), dtype),
            jax.ShapeDtypeStruct((nt, nw, cap, 2, slots, blk, blk), dtype),
            jax.ShapeDtypeStruct((nt, *down.shape), dtype),
            jax.ShapeDtypeStruct(rows.shape, rows.dtype),
        ),
        in_specs=[pl.BlockSpec(memory_space=pltpu.SMEM), any_spec, any_spec, any_spec, any_spec, any_spec],
        out_specs=(any_spec,) * 4,
        scratch_shapes=[
            pltpu.VMEM(gate.shape, dtype),
            pltpu.VMEM(up.shape, dtype),
            pltpu.VMEM((nw, cap, 2, slots, blk, blk), dtype),
            pltpu.VMEM((row_count, blk), dtype),
            sem((zs - 1,)), sem((zs - 1,)), sem((zs - 1,)), sem((zs - 1,)),
            sem((zs, ys - 1)), sem((zs, ys - 1)),
            sem((nw - 1,)), sem((nw - 1,)), sem((nw - 1,)), sem((nw - 1,)),
            sem((nw + 1, xs - 1)), sem((nw + 1, xs - 1)), sem((nw + 1, xs)), sem((nw + 1, xs)),
            sem((7,)),
        ],
        compiler_params=pltpu.CompilerParams(
            collective_id=0, has_side_effects=True, vmem_limit_bytes=60 << 20
        ),
    )(ids, rows, tokens, gate, up, down)


def layer_kernel(sizes, rows_ref, places_ref, feat_ref, got_ref, down_hbm, out_ref, hidden, down_ref, down_sem):
    nt, nw, cap, kg, kd, none = sizes
    step = pl.program_id(0)
    blk = feat_ref.shape[2]

    load = pltpu.make_async_copy(down_hbm, down_ref, down_sem)

    def column(s, which):
        base = ((step * cap + s) * 2 + which) * kg
        lhs = jnp.concatenate([feat_ref[rows_ref[base + k]] for k in range(kg)], axis=1)
        rhs = jnp.concatenate([got_ref[tt, 0, s, which].reshape(-1, blk) for tt in range(nt)], axis=0)
        return jnp.dot(lhs, rhs, preferred_element_type=jnp.float32)

    @pl.when(step == 0)
    def _():
        load.start()
        hidden[nw * cap] = jnp.zeros(hidden.shape[1:], hidden.dtype)

    for s in range(cap):
        gate = column(s, 0)
        up = column(s, 1)
        hidden[step * cap + s] = (gate / (1.0 + jnp.exp(-gate)) * up).astype(hidden.dtype)

    @pl.when(step == nw - 1)
    def _():
        load.wait()
        for b in range(out_ref.shape[1] // blk):
            lhs = jnp.concatenate([hidden[places_ref[b * kd + k]] for k in range(kd)], axis=1)
            rhs = jnp.concatenate([down_ref[tt, b].reshape(-1, blk) for tt in range(nt)], axis=0)
            out_ref[:, b * blk : (b + 1) * blk] = jnp.dot(
                lhs, rhs, preferred_element_type=jnp.float32
            ).astype(out_ref.dtype)


def layer(sizes, rows, places, feat, got, down):
    nt, nw, cap, kg, kd, none = sizes
    row_count, blk = feat.shape[1:]
    outs = down.shape[1]
    vmem_spec = pl.BlockSpec(memory_space=pltpu.VMEM)
    return pl.pallas_call(
        functools.partial(layer_kernel, sizes),
        out_shape=jax.ShapeDtypeStruct((row_count, outs * blk), feat.dtype),
        grid_spec=pltpu.PrefetchScalarGridSpec(
            num_scalar_prefetch=2,
            grid=(nw,),
            in_specs=[
                vmem_spec,
                pl.BlockSpec((nt, 1, *got.shape[2:]), lambda i, a, b: (0, i, 0, 0, 0, 0, 0)),
                pl.BlockSpec(memory_space=pl.ANY),
            ],
            out_specs=pl.BlockSpec((row_count, outs * blk), lambda i, a, b: (0, 0)),
            scratch_shapes=[
                pltpu.VMEM((nw * cap + 1, row_count, blk), feat.dtype),
                pltpu.VMEM(down.shape, down.dtype),
                pltpu.SemaphoreType.DMA,
            ],
        ),
        compiler_params=pltpu.CompilerParams(vmem_limit_bytes=58 << 20),
    )(rows, places, feat, got, down)


def running(flags):
    upto = jnp.arange(flags.shape[1])
    upto = upto[:, None] >= upto[None, :]
    return jnp.sum((flags[:, None, :] & upto[None]).astype(jnp.int32), axis=2)


def on_device(tokens, gate_weight, up_weight, down_weight, gate_list, up_list, down_list):
    nt, nw = lax.axis_size("tok"), lax.axis_size("wa")
    me = lax.axis_index("wa")
    hid_blocks, _, blk, _ = gate_weight.shape
    outs = down_weight.shape[0]
    kd, kg = down_list.shape[1], gate_list.shape[1]
    cap = max(2, (kd + nw - 1) // nw + 1)
    row_count = tokens.shape[0]
    fb = tokens.shape[1] // blk
    groups = down_list.reshape(nw, -1)

    own_ids = me * hid_blocks + jnp.arange(hid_blocks, dtype=jnp.int32)
    wanted = jnp.any(groups[:, :, None] == own_ids[None, None, :], axis=1)
    places = running(wanted) - 1
    chosen = wanted[:, None, :] & (places[:, None, :] == jnp.arange(cap, dtype=jnp.int32)[None, :, None])
    ids = jnp.sum(jnp.where(chosen, jnp.arange(hid_blocks, dtype=jnp.int32), 0), axis=2)
    both = jnp.concatenate([gate_list, up_list], axis=1)
    both = jnp.where(both < 0, nw * fb, both)
    picked = jnp.sum(jnp.where(chosen[..., None], both[None, None], 0), axis=2).reshape(nw, -1)
    width = -(-picked.shape[1] // 1024) * 1024
    rows = jnp.pad(picked, ((0, 0), (0, width - picked.shape[1]))).reshape(nw, -1, 128)

    mine = lax.dynamic_slice_in_dim(down_list, me * outs, outs, 0)
    all_ids = jnp.arange(nw * hid_blocks, dtype=jnp.int32)
    hit = mine.reshape(-1)[:, None] == all_ids[None, :]
    named = jnp.any(hit, axis=0).reshape(nw, hid_blocks)
    spot = running(named) - 1 + cap * jnp.arange(nw, dtype=jnp.int32)[:, None]
    spots = jnp.sum(jnp.where(hit, spot.reshape(1, -1), 0), axis=1)
    spots = jnp.where(mine.reshape(-1) >= 0, spots, nw * cap)

    blocks = jnp.transpose(tokens.reshape(row_count, fb, blk), (1, 0, 2))
    feat, got, down, got_rows = exchange(
        (nt, nw, cap), ids.reshape(-1), rows, blocks, gate_weight, up_weight, down_weight
    )
    lists = got_rows.reshape(nw, -1)[:, : cap * 2 * kg].reshape(-1)
    return layer((nt, nw, cap, kg, kd, nw * fb), lists, spots, feat, got, down)


def solution(mesh):
    placed = (
        P("tok", "wa"),
        P("wa", "tok", None, None),
        P("wa", "tok", None, None),
        P("wa", "tok", None, None),
        P("wa", None),
        P("wa", None),
        P(),
    )
    return jax.shard_map(
        on_device, mesh=mesh, in_specs=placed, out_specs=P("tok", "wa"), check_vma=False
    )
```
